32 devices in a mesh: segment: 4 (over y, x), ctx: 8 (over z, core).
Axes of the slice: x: 2, y: 2, z: 4, core: 2. Of those that a mesh axis runs over, the one named last changes fastest.
Arguments:
- queries: bfloat16 [4, 8, 2048, 2048], P('segment', None, 'ctx'), may hold values from -3 to 3
- keys: bfloat16 [4, 8, 2048, 512], P('segment', None, 'ctx'), may hold values from -3 to 3
- values: bfloat16 [4, 8, 2048, 512], P('segment', None, 'ctx'), may hold values from -6 to 6
- grad_slab: bfloat16 [4, 2048, 2048], P('segment', 'ctx'), may hold values from -6 to 6
- plan: int32 [4], P('segment'), may hold values from 0 to 7
- random_blocks: int32 [16, 3], replicated, may hold values from 1 to 15, as said below
Outputs:
- query_grad: bfloat16 [4, 2048, 2048], P('segment', 'ctx')
- key_grad: bfloat16 [4, 2048, 512], P('segment', 'ctx')
- value_grad: bfloat16 [4, 2048, 512], P('segment', 'ctx')
The draws below stay inside these ranges and needn't reach their ends.
Inputs may be any that keep to these rules, and one draw needn't show every extreme that they name: `random_blocks`: each row b holds 3 different block numbers, none equal to b - 1, b, b + 1 (mod 16) or to 0.
All inputs are finite; a program needn't handle non-finite values.
Results may differ from the reference program's by a relative error of at most 0.012.
Values may be sent and summed in bfloat16 or wider, within the bound.
A program may use at most 192 MiB of HBM per device.

```python
import jax
import jax.numpy as jnp
from jax import lax

HQ = 16
HK = 4
HD = 128
BLK = 128
NR = 3
MB = 8
SEQ = 2048
NQB = 16
SEGMENTS = 4


def draw_random_blocks(key, part):
    block_ids = jnp.arange(NQB, dtype=jnp.int32)
    row_ids = block_ids[:, None]
    column_ids = block_ids[None, :]
    excluded = (column_ids == row_ids) | (column_ids == (row_ids + 1) % NQB) | (column_ids == (row_ids - 1) % NQB) | (column_ids == 0)
    raw_scores = jax.random.randint(jax.random.fold_in(key, 12), (NQB, NQB), 0, 1 << 16).astype(jnp.int32)
    distinct = raw_scores * NQB + column_ids
    distinct = jnp.where(excluded, -1, distinct)
    top_scores, top_ids = jax.lax.top_k(distinct, NR)
    return top_ids.astype(jnp.int32)


def with_ends(result, key, least, high):
    extent = result.shape
    index_at = [jax.random.randint(jax.random.fold_in(key, axis), (), 0, extent[axis]) for axis in range(len(extent))]
    result = result.at[tuple(index_at)].set(least)
    longest = extent.index(max(extent))
    index_at[longest] = (index_at[longest] + 1) % extent[longest]
    return result.at[tuple(index_at)].set(high)


def block_scale(key, shape, cuts, smallest, top_value):
    loudness = 1.0
    for dim, blocks in cuts:
        heights = jax.random.uniform(jax.random.fold_in(jax.random.fold_in(key, 6), dim), (blocks,), jnp.float32, smallest / len(cuts), top_value / len(cuts))
        loudness = loudness * jnp.repeat(jnp.exp(heights), shape[dim] // blocks).reshape((-1,) + (1,) * (len(shape) - 1 - dim))
    return loudness


def noise(stream_key, extent, scale, reach, cuts=(), kind=jnp.bfloat16):
    array = scale * jax.random.normal(stream_key, extent, jnp.float32)
    if cuts:
        array = array * block_scale(stream_key, extent, cuts, -0.22, 0.18)
    return jnp.clip(array, -reach, reach).astype(kind)


def setup_inputs(seed: int = 0) -> dict:
    key_of = jax.random.split(jax.random.key(seed), 7)
    return {
        "queries": noise(key_of[0], (SEGMENTS, MB, SEQ, HQ * HD), 1.0, 3.0, ((0, 4), (2, 8))),
        "keys": noise(key_of[1], (SEGMENTS, MB, SEQ, HK * HD), 1.0, 3.0, ((0, 4), (2, 8))),
        "values": noise(key_of[2], (SEGMENTS, MB, SEQ, HK * HD), 1.0, 6.0, ((0, 4), (2, 8))),
        "grad_slab": noise(key_of[3], (SEGMENTS, SEQ, HQ * HD), 1.0, 6.0, ((0, 4), (1, 8))),
        "plan": with_ends(jax.random.randint(key_of[4], (SEGMENTS,), 0, MB), jax.random.fold_in(key_of[4], 1), 0, MB - 1).astype(jnp.int32),
        "random_blocks": draw_random_blocks(jax.random.fold_in(key_of[6], 71), 0),
    }


def make_mask(random_blocks):
    block_ids = jnp.arange(NQB, dtype=jnp.int32)
    column_ids = block_ids[None, :]
    row_ids = block_ids[:, None]
    nearby = (column_ids == row_ids) | (column_ids == (row_ids + 1) % NQB) | (column_ids == (row_ids - 1) % NQB)
    chosen = jnp.any(random_blocks[:, :, None] == column_ids[:, None, :], axis=1)
    allowed = nearby | chosen | (column_ids == 0) | (row_ids == 0)
    return allowed.astype(jnp.float32)


def reference(queries, keys, values, grad_slab, plan, random_blocks):
    block_mask = make_mask(random_blocks)
    token_mask = jnp.repeat(jnp.repeat(block_mask, BLK, axis=0), BLK, axis=1)
    score_scale = HD ** -0.5
    group_size = HQ // HK

    def one_segment(segment_id):
        chosen_mb = plan[segment_id]
        query_all = queries[segment_id, chosen_mb]
        key_all = keys[segment_id, chosen_mb]
        value_all = values[segment_id, chosen_mb]
        upstream = grad_slab[(segment_id + 1) % SEGMENTS]

        def one_head(head_id):
            kv_head = head_id // group_size
            head_query = lax.dynamic_slice_in_dim(query_all, head_id * HD, HD, 1)
            head_grad = lax.dynamic_slice_in_dim(upstream, head_id * HD, HD, 1)
            head_key = lax.dynamic_slice_in_dim(key_all, kv_head * HD, HD, 1)
            head_value = lax.dynamic_slice_in_dim(value_all, kv_head * HD, HD, 1)
            scores = jnp.dot(head_query, head_key.T, preferred_element_type=jnp.float32) * score_scale
            exp_scores = jnp.exp(scores) * token_mask
            totals = jnp.sum(exp_scores, axis=1)
            weights = exp_scores / totals[:, None]
            weights_low = weights.astype(jnp.bfloat16)
            dprobs = jnp.dot(head_grad, head_value.T, preferred_element_type=jnp.float32)
            deltas = jnp.sum(weights_low.astype(jnp.float32) * dprobs, axis=1)
            dscore = (weights * (dprobs - deltas[:, None])).astype(jnp.bfloat16)
            dquery = score_scale * jnp.dot(dscore, head_key, preferred_element_type=jnp.float32)
            key_term = score_scale * jnp.dot(dscore.T, head_query, preferred_element_type=jnp.float32)
            value_term = jnp.dot(weights_low.T, head_grad, preferred_element_type=jnp.float32)
            return dquery, key_term, value_term

        dquery, key_term, value_term = lax.map(one_head, jnp.arange(HQ, dtype=jnp.int32))
        query_out = dquery.transpose(1, 0, 2).reshape(SEQ, HQ * HD).astype(jnp.bfloat16)
        key_out = key_term.reshape(HK, group_size, SEQ, HD).sum(axis=1).transpose(1, 0, 2).reshape(SEQ, HK * HD)
        value_out = value_term.reshape(HK, group_size, SEQ, HD).sum(axis=1).transpose(1, 0, 2).reshape(SEQ, HK * HD)
        return query_out, key_out.astype(jnp.bfloat16), value_out.astype(jnp.bfloat16)

    query_grad, key_grad, value_grad = lax.map(one_segment, jnp.arange(SEGMENTS, dtype=jnp.int32))
    return (query_grad, key_grad, value_grad)
```

```python
import functools

import jax
import jax.numpy as jnp
from jax import lax
from jax.experimental import pallas as pl
from jax.experimental.pallas import tpu as pltpu
from jax.sharding import PartitionSpec as P

HD = 128
BLK = 128
GROUP = 4
NSLOT = 7
LOG2E = 1.4426950408889634
MESH = pl.DeviceIdType.MESH


def dot(a, b, ca, cb):
    return lax.dot_general(a, b, (((ca,), (cb,)), ((), ())), preferred_element_type=jnp.float32)


def kernel(
    n_seg, nz, rb_ref, q_in, g_in, kv_in, dq_out, kv_out,
    q0, q1, g0, g1, kv0, kv1, slk0, slk1, slv0, slv1,
    rr0, rr1, rl0, rl1, dq0, dq1, fin0, fin1,
    kgat, vgat, dsb, pbb, tab,
    swap_s, swap_r, grad_s, grad_r, ga_s, ga_r, rs_s, rs_r, out_s, out_r,
):
    seg = lax.axis_index("segment")
    ctx = lax.axis_index("ctx")
    z = ctx // 2
    core = ctx % 2
    other = 1 - core
    nb = nz * 4
    q_sc, g_sc, kv_sc = (q0, q1), (g0, g1), (kv0, kv1)
    slk, slv = (slk0, slk1), (slv0, slv1)
    rs_buf = ((rr0, rl0), (rr1, rl1))
    dq_sc, fin = (dq0, dq1), (fin0, fin1)
    scale = HD ** (-0.5)
    partner = (seg, ctx + 1 - 2 * core)
    right = (seg, ctx + 2)
    left = (seg, ctx - 2)
    ahead = lax.rem(seg + 1, n_seg)
    behind = lax.rem(seg + n_seg - 1, n_seg)
    has_left, has_right = z > 0, z < nz - 1

    def rcopy(src, dst, ss, rs, dev):
        return pltpu.make_async_remote_copy(
            src_ref=src, dst_ref=dst, send_sem=ss, recv_sem=rs, device_id=dev, device_id_type=MESH
        )

    barrier = pltpu.get_barrier_semaphore()
    for dev in (
        partner, (ahead, z * 2), (ahead, z * 2 + 1), (behind, z * 2), (behind, z * 2 + 1)
    ):
        pl.semaphore_signal(barrier, inc=1, device_id=dev, device_id_type=MESH)

    @pl.when(has_left)
    def _():
        pl.semaphore_signal(barrier, inc=1, device_id=left, device_id_type=MESH)

    @pl.when(has_right)
    def _():
        pl.semaphore_signal(barrier, inc=1, device_id=right, device_id_type=MESH)

    pl.semaphore_wait(barrier, 5 + has_left.astype(jnp.int32) + has_right.astype(jnp.int32))

    def swap_kv(h):
        return rcopy(
            kv_in.at[other * 2 + h], kv_sc[h].at[pl.ds(z * 8 + core * 4, 4)],
            swap_s.at[0, h], swap_r.at[0, h], partner,
        )

    def swap_q(h):
        return rcopy(
            q_in.at[other * 2 + h], q_sc[h].at[pl.ds(core * 2, 2)],
            swap_s.at[1, h], swap_r.at[1, h], partner,
        )

    def hand_off(h, c):
        return rcopy(
            g_in.at[c * 2 + h], g_sc[h].at[pl.ds(core * 2, 2)],
            grad_s.at[h, c], grad_r.at[h, core], (behind, z * 2 + c),
        )

    def hand_off_in(h, c):
        part = g_sc[h].at[pl.ds(c * 2, 2)]
        return rcopy(part, part, grad_s.at[h, c], grad_r.at[h, c], (ahead, z * 2 + c))

    def chunk_copy(h, d, j):
        part = kv_sc[h].at[pl.ds(j * 8, 8)]
        return rcopy(part, part, ga_s.at[h, d, j], ga_r.at[h, j], left if d else right)

    def send_own(h):
        @pl.when(has_right)
        def _():
            chunk_copy(h, 0, z).start()

        @pl.when(has_left)
        def _():
            chunk_copy(h, 1, z).start()

    def hop(h, dist):
        @pl.when(z >= dist)
        def _():
            chunk_copy(h, 0, z - dist).wait_recv()

            @pl.when(has_right)
            def _():
                chunk_copy(h, 0, z - dist).start()

        @pl.when(z + dist <= nz - 1)
        def _():
            chunk_copy(h, 1, z + dist).wait_recv()

            @pl.when(has_left)
            def _():
                chunk_copy(h, 1, z + dist).start()

    def hop_sends(h):
        for dist in range(nz):
            @pl.when((z >= dist) & has_right)
            def _():
                chunk_copy(h, 0, z - dist).wait_send()

            @pl.when((z + dist <= nz - 1) & has_left)
            def _():
                chunk_copy(h, 1, z + dist).wait_send()

    for h in range(2):
        swap_kv(h).start()
    for h in range(2):
        for c in range(2):
            hand_off(h, c).start()
        swap_q(h).start()

    for h in range(2):
        kv_sc[h][pl.ds(z * 8 + core * 4, 4)] = kv_in[core * 2 + h]
        q_sc[h][pl.ds(core * 2, 2)] = q_in[core * 2 + h]

    swap_kv(0).wait_recv()
    send_own(0)

    for h in range(2):
        slk[h][NSLOT] = jnp.zeros((BLK, HD), jnp.float32)
        slv[h][NSLOT] = jnp.zeros((BLK, HD), jnp.float32)

    def slots(r):
        b = z * 4 + r
        ids = [lax.rem(b + nb - 1, nb), b, lax.rem(b + 1, nb), 0]
        ids += [rb_ref[b * 3 + i] for i in range(3)]
        extra = (b != 0) & (b != 1) & (b != nb - 1)
        return b, ids, extra

    def fill(c, _):
        for r in range(4):
            b, ids, extra = slots(r)
            where = jnp.where(extra & (c == 0), r * 8 + 3, NSLOT)
            for s in (0, 1, 2, 4, 5, 6):
                where = jnp.where(ids[s] == c, r * 8 + s, where)
            tab[r * nb + c] = jnp.where(b == 0, 32 + c, where)
        return 0

    lax.fori_loop(0, nb, fill, 0)

    def attend(h, r, n, base, extra):
        width = n * BLK
        if extra is not None:
            lane = lax.broadcasted_iota(jnp.int32, (1, width), 1) // BLK
            keep = jnp.where(lane == 3, extra.astype(jnp.float32), 1.0)

        def head(g):
            query, grad = q_sc[h][r, g], g_sc[h][r, g]
            exp_s = jnp.exp2(dot(query, kgat[:width], 1, 1) * (scale * LOG2E))
            if extra is not None:
                exp_s = exp_s * keep
            total = jnp.sum(exp_s, axis=1, keepdims=True)
            shrink = jnp.where(total > 1.0, 2.0**-8, 1.0)
            p = (exp_s * shrink) * (1.0 / (total * shrink))
            p_low = p.astype(jnp.bfloat16)
            dp = dot(grad, vgat[:width], 1, 1)
            delta = jnp.sum(p_low.astype(jnp.float32) * dp, axis=1, keepdims=True)
            ds = (p * (dp - delta)).astype(jnp.bfloat16)
            rows = pl.ds(pl.multiple_of(g * BLK, BLK), BLK)
            pbb[rows, :width] = p_low
            dsb[rows, :width] = ds
            dq = dot(ds, kgat[:width], 1, 0) * scale
            dq_sc[h][r, g] = dq.astype(jnp.bfloat16)

        if extra is None:
            @pl.loop(0, GROUP)
            def _(g):
                head(g)
        else:
            for g in range(GROUP):
                head(g)
        q_t = q_sc[h][r].reshape(GROUP * BLK, HD).T
        g_t = g_sc[h][r].reshape(GROUP * BLK, HD).T
        dk = dot(q_t, dsb[:, :width], 1, 0)
        for s in range(n):
            slk[h][base + s] = dk[:, s * BLK:(s + 1) * BLK]
        dv = dot(g_t, pbb[:, :width], 1, 0)
        for s in range(n):
            slv[h][base + s] = dv[:, s * BLK:(s + 1) * BLK]

    def row(h, r):
        b, ids, extra = slots(r)

        @pl.when(b == 0)
        def _():
            for c in range(nb):
                tile = (c // 2) * 4 + c % 2
                kgat[c * BLK:(c + 1) * BLK] = kv_sc[h][tile]
                vgat[c * BLK:(c + 1) * BLK] = kv_sc[h][tile + 2]
            attend(h, r, nb, 32, None)

        @pl.when(b != 0)
        def _():
            for s in range(NSLOT):
                tile = (ids[s] >> 1) * 4 + (ids[s] & 1)
                kgat[s * BLK:(s + 1) * BLK] = kv_sc[h][tile]
                vgat[s * BLK:(s + 1) * BLK] = kv_sc[h][tile + 2]
            attend(h, r, NSLOT, r * 8, extra)

    def rows(h, first, last):
        @pl.loop(first, last)
        def _(r):
            row(h, r)

    def terms(h, j, m):
        c = j * 4 + m
        at = [tab[r * nb + c] for r in range(4)]
        dk = (slk[h][at[0]] + slk[h][at[1]]) + (slk[h][at[2]] + slk[h][at[3]])
        dv = (slv[h][at[0]] + slv[h][at[1]]) + (slv[h][at[2]] + slv[h][at[3]])
        return dk, dv

    def sum_copy(h, d, j):
        part = rs_buf[h][d].at[pl.ds(j * 8, 8)]
        return rcopy(part, part, rs_s.at[h, d, j], rs_r.at[h, d, j], left if d else right)

    def add_own(h, d, j, first):
        buf = rs_buf[h][d]

        @pl.loop(0, 4)
        def _(m):
            dk, dv = terms(h, j, m)
            k = j * 8 + (m // 2) * 4 + m % 2
            if not first:
                dk = dk + buf[k].astype(jnp.float32)
                dv = dv + buf[k + 2].astype(jnp.float32)
            buf[k] = dk.astype(jnp.bfloat16)
            buf[k + 2] = dv.astype(jnp.bfloat16)

    def sum_step(h, t):
        for d in range(2):
            i = nz - 1 - z if d else z
            to = i + nz - 1 - t
            j = nz - 1 - to if d else to

            @pl.when(i == 0)
            def _():
                add_own(h, d, j, True)
                sum_copy(h, d, j).start()

            if t:
                @pl.when((i > 0) & (i <= t))
                def _():
                    sum_copy(h, d, j).wait_recv()
                    add_own(h, d, j, False)
                    sum_copy(h, d, j).start()

    def sum_sends(h):
        for t in range(nz - 1):
            for d in range(2):
                i = nz - 1 - z if d else z
                to = i + nz - 1 - t
                j = nz - 1 - to if d else to

                @pl.when(i <= t)
                def _():
                    sum_copy(h, d, j).wait_send()

    def kv_back(h):
        return rcopy(
            fin[h].at[other], kv_out.at[core * 2 + h], out_s.at[0, h], out_r.at[0, h], partner
        )

    def dq_back(h):
        return rcopy(
            dq_sc[h].at[pl.ds(other * 2, 2)], dq_out.at[core * 2 + h],
            out_s.at[1, h], out_r.at[1, h], partner,
        )

    def finish(h):
        @pl.when(has_left)
        def _():
            sum_copy(h, 0, z).wait_recv()

        @pl.when(has_right)
        def _():
            sum_copy(h, 1, z).wait_recv()

        from_left = has_left.astype(jnp.float32)
        from_right = has_right.astype(jnp.float32)

        @pl.loop(0, 4)
        def _(m):
            dk, dv = terms(h, z, m)
            k = (m // 2) * 4 + m % 2
            parts = []
            for total, e in ((dk, 0), (dv, 2)):
                at_left = rs_buf[h][0][z * 8 + k + e].astype(jnp.float32)
                at_right = rs_buf[h][1][z * 8 + k + e].astype(jnp.float32)
                total = total + jnp.where(from_left > 0, at_left, 0.0)
                parts.append(total + jnp.where(from_right > 0, at_right, 0.0))
            fin[h][m // 2, m % 2] = (parts[0].T * scale).astype(jnp.bfloat16)
            fin[h][m // 2, m % 2 + 2] = parts[1].T.astype(jnp.bfloat16)

        kv_back(h).start()
        kv_out[core * 2 + h] = fin[h][core]

    for dist in range(1, nz):
        hop(0, dist)
        if dist == max(nz - 2, 1):
            swap_kv(1).wait_recv()
            send_own(1)
    hop(1, 1)
    for h in range(2):
        swap_q(h).wait_recv()
    for c in range(2):
        hand_off_in(0, c).wait_recv()
    rows(0, 0, 2)
    for dist in range(2, nz - 1):
        hop(1, dist)
    rows(0, 2, 4)
    if nz > 2:
        hop(1, nz - 1)
    for c in range(2):
        hand_off_in(1, c).wait_recv()
    sum_step(0, 0)
    dq_back(0).start()
    rows(1, 0, 2)
    for t in range(1, nz - 2):
        sum_step(0, t)
    rows(1, 2, 4)
    if nz > 2:
        sum_step(0, nz - 2)
    sum_step(1, 0)
    dq_back(1).start()
    for h in range(2):
        dq_out[core * 2 + h] = dq_sc[h][pl.ds(core * 2, 2)]
    finish(0)
    for t in range(1, nz - 1):
        sum_step(1, t)
    finish(1)

    for h in range(2):
        swap_kv(h).wait_send()
        swap_q(h).wait_send()
        for c in range(2):
            hand_off(h, c).wait_send()
        hop_sends(h)
        sum_sends(h)
        dq_back(h).wait()
        kv_back(h).wait()


def per_device(n_seg, n_ctx, queries, keys, values, grad_slab, plan, random_blocks):
    nz = n_ctx // 2
    nb = nz * 4
    mb = plan[0]
    query_now = lax.dynamic_index_in_dim(queries[0], mb, 0, keepdims=False)
    key_now = lax.dynamic_index_in_dim(keys[0], mb, 0, keepdims=False)
    value_now = lax.dynamic_index_in_dim(values[0], mb, 0, keepdims=False)
    q_in = query_now.reshape(2, BLK, 4, GROUP, HD).transpose(2, 0, 3, 1, 4)
    g_in = grad_slab[0].reshape(2, BLK, 4, GROUP, HD).transpose(2, 0, 3, 1, 4)
    kv_in = jnp.concatenate(
        [
            key_now.reshape(2, BLK, 4, HD).transpose(2, 0, 1, 3),
            value_now.reshape(2, BLK, 4, HD).transpose(2, 0, 1, 3),
        ],
        axis=1,
    )
    low = jnp.bfloat16
    vmem = pl.BlockSpec(memory_space=pltpu.VMEM)
    dma = pltpu.SemaphoreType.DMA
    rows4 = pltpu.VMEM((4, GROUP, BLK, HD), low)
    line = pltpu.VMEM((nb * 2, BLK, HD), low)
    tiles = pltpu.VMEM((32 + nb, BLK, HD), jnp.float32)
    dq, dkv = pl.pallas_call(
        functools.partial(kernel, n_seg, nz),
        out_shape=(
            jax.ShapeDtypeStruct((4, 2, GROUP, BLK, HD), low),
            jax.ShapeDtypeStruct((4, 4, BLK, HD), low),
        ),
        in_specs=[pl.BlockSpec(memory_space=pltpu.SMEM), vmem, vmem, vmem],
        out_specs=(vmem, vmem),
        scratch_shapes=[
            rows4, rows4, rows4, rows4, line, line, tiles, tiles, tiles, tiles,
            line, line, line, line, rows4, rows4,
            pltpu.VMEM((2, 4, BLK, HD), low), pltpu.VMEM((2, 4, BLK, HD), low),
            pltpu.VMEM((nb * BLK, HD), low), pltpu.VMEM((nb * BLK, HD), low),
            pltpu.VMEM((GROUP * BLK, nb * BLK), low), pltpu.VMEM((GROUP * BLK, nb * BLK), low),
            pltpu.SMEM((4 * nb,), jnp.int32),
            dma((2, 2)), dma((2, 2)), dma((2, 2)), dma((2, 2)),
            dma((2, 2, nz)), dma((2, nz)), dma((2, 2, nz)), dma((2, 2, nz)),
            dma((2, 2)), dma((2, 2)),
        ],
        compiler_params=pltpu.CompilerParams(
            collective_id=0, has_side_effects=True, vmem_limit_bytes=60 * 1024 * 1024
        ),
        cost_estimate=pl.CostEstimate(
            flops=6_000_000_000, bytes_accessed=8_000_000, transcendentals=6_000_000
        ),
    )(random_blocks.reshape(-1), q_in, g_in, kv_in)
    query_grad = dq.transpose(1, 3, 0, 2, 4).reshape(1, 2 * BLK, -1)
    key_grad = dkv[:, :2].transpose(1, 2, 0, 3).reshape(1, 2 * BLK, -1)
    value_grad = dkv[:, 2:].transpose(1, 2, 0, 3).reshape(1, 2 * BLK, -1)
    return (query_grad, key_grad, value_grad)


def solution(mesh):
    return jax.shard_map(
        functools.partial(per_device, mesh.shape["segment"], mesh.shape["ctx"]),
        mesh=mesh,
        in_specs=(
            P("segment", None, "ctx", None),
            P("segment", None, "ctx", None),
            P("segment", None, "ctx", None),
            P("segment", "ctx", None),
            P("segment"),
            P(),
        ),
        out_specs=(P("segment", "ctx", None), P("segment", "ctx", None), P("segment", "ctx", None)),
        check_vma=False,
    )
```

```python
import functools

import jax
import jax.numpy as jnp
from jax import lax
from jax.experimental import pallas as pl
from jax.experimental.pallas import tpu as pltpu
from jax.sharding import PartitionSpec as P

HD = 128
BLK = 128
GROUP = 4
NSLOT = 7
LOG2E = 1.4426950408889634
MESH = pl.DeviceIdType.MESH


def dot(a, b, ca, cb):
    return lax.dot_general(a, b, (((ca,), (cb,)), ((), ())), preferred_element_type=jnp.float32)


def kernel(
    n_seg, nz, rb_ref, q_in, g_in, k_in, v_in, dq_out, dk_out, dv_out,
    q_sc, g_sc, dq_sc, k0, v0, k1, v1, slv0, slk0, slv1, slk1, sums, fin,
    kgat, vgat, s_ref, dsb, p_plain, p_full, tab,
    swap_s, swap_r, qs_s, qs_r, grad_s, grad_r, ga_s, ga_r, rs_s, rs_r,
    dq_s, dq_r, out_s, out_r,
):
    seg = lax.axis_index("segment")
    ctx = lax.axis_index("ctx")
    z = ctx // 2
    core = ctx % 2
    other = 1 - core
    nb = nz * 4
    line = (k0, v0, k1, v1)
    terms_of = (slv0, slk0, slv1, slk1)
    scale = HD ** (-0.5)
    partner = (seg, ctx + 1 - 2 * core)
    right = (seg, ctx + 2)
    left = (seg, ctx - 2)
    ahead = lax.rem(seg + 1, n_seg)
    behind = lax.rem(seg + n_seg - 1, n_seg)
    has_left, has_right = z > 0, z < nz - 1

    def rcopy(src, dst, ss, rs, dev):
        return pltpu.make_async_remote_copy(
            src_ref=src, dst_ref=dst, send_sem=ss, recv_sem=rs, device_id=dev, device_id_type=MESH
        )

    def cols(at):
        return pl.ds(pl.multiple_of(at * HD, HD), HD)

    def block(b):
        return pl.ds(b * BLK, BLK)

    barrier = pltpu.get_barrier_semaphore()
    for dev in (
        partner, (ahead, z * 2), (ahead, z * 2 + 1), (behind, z * 2), (behind, z * 2 + 1)
    ):
        pl.semaphore_signal(barrier, inc=1, device_id=dev, device_id_type=MESH)

    @pl.when(has_left)
    def _():
        pl.semaphore_signal(barrier, inc=1, device_id=left, device_id_type=MESH)

    @pl.when(has_right)
    def _():
        pl.semaphore_signal(barrier, inc=1, device_id=right, device_id_type=MESH)

    pl.semaphore_wait(barrier, 5 + has_left.astype(jnp.int32) + has_right.astype(jnp.int32))

    def swap_kv(u):
        source = v_in if u % 2 else k_in
        for b in range(2):
            rcopy(
                source.at[block(b), cols(other * 2 + u // 2)], line[u].at[z * 4 + core * 2 + b],
                swap_s.at[u], swap_r.at[u], partner,
            ).start()

    def swap_kv_all(u):
        part = line[u].at[pl.ds(z * 4 + other * 2, 2)]
        return rcopy(part, part, swap_s.at[u], swap_r.at[u], partner)

    def swap_q(h):
        for b in range(2):
            for g in range(GROUP):
                rcopy(
                    q_in.at[block(b), cols((other * 2 + h) * GROUP + g)],
                    q_sc.at[h, core * 2 + b, g], qs_s.at[h], qs_r.at[h], partner,
                ).start()

    def swap_q_all(h):
        part = q_sc.at[h, pl.ds(other * 2, 2)]
        return rcopy(part, part, qs_s.at[h], qs_r.at[h], partner)

    def hand_off(h):
        for c in range(2):
            for b in range(2):
                for g in range(GROUP):
                    rcopy(
                        g_in.at[0, block(b), cols((c * 2 + h) * GROUP + g)],
                        g_sc.at[h, core * 2 + b, g],
                        grad_s.at[h, c], grad_r.at[h, core], (behind, z * 2 + c),
                    ).start()

    def hand_off_all(h, c):
        part = g_sc.at[h, pl.ds(c * 2, 2)]
        return rcopy(part, part, grad_s.at[h, c], grad_r.at[h, c], (ahead, z * 2 + c))

    def chunk_copy(u, d, j):
        part = line[u].at[pl.ds(j * 4, 4)]
        return rcopy(part, part, ga_s.at[u, d, j], ga_r.at[u, j], left if d else right)

    def send_own(u):
        swap_kv_all(u).wait_recv()

        @pl.when(has_right)
        def _():
            chunk_copy(u, 0, z).start()

        @pl.when(has_left)
        def _():
            chunk_copy(u, 1, z).start()

    def hop(u, dist):
        @pl.when(z >= dist)
        def _():
            chunk_copy(u, 0, z - dist).wait_recv()

            @pl.when(has_right)
            def _():
                chunk_copy(u, 0, z - dist).start()

        @pl.when(z + dist <= nz - 1)
        def _():
            chunk_copy(u, 1, z + dist).wait_recv()

            @pl.when(has_left)
            def _():
                chunk_copy(u, 1, z + dist).start()

    def hop_sends(u):
        for dist in range(nz):
            @pl.when((z >= dist) & has_right)
            def _():
                chunk_copy(u, 0, z - dist).wait_send()

            @pl.when((z + dist <= nz - 1) & has_left)
            def _():
                chunk_copy(u, 1, z + dist).wait_send()

    swap_kv(0)
    hand_off(0)
    swap_q(0)
    for u in range(4):
        source = v_in if u % 2 else k_in
        if u:
            swap_kv(u)
        for b in range(2):
            line[u][z * 4 + core * 2 + b] = source[block(b), cols(core * 2 + u // 2)]
        if u == 0:
            send_own(0)
    swap_q(1)
    for h in range(2):
        for b in range(2):
            for g in range(GROUP):
                q_sc[h, core * 2 + b, g] = q_in[block(b), cols((core * 2 + h) * GROUP + g)]

    for u in range(4):
        terms_of[u][NSLOT] = jnp.zeros((BLK, HD), jnp.float32)

    def slots(r):
        b = z * 4 + r
        ids = [lax.rem(b + nb - 1, nb), b, lax.rem(b + 1, nb), 0]
        ids += [rb_ref[b, i] for i in range(3)]
        extra = (b != 0) & (b != 1) & (b != nb - 1)
        return b, ids, extra

    def fill(c, _):
        for r in range(4):
            b, ids, extra = slots(r)
            where = jnp.where(extra & (c == 0), r * 8 + 3, NSLOT)
            for s in (0, 1, 2, 4, 5, 6):
                where = jnp.where(ids[s] == c, r * 8 + s, where)
            tab[r * nb + c] = jnp.where(b == 0, 32 + c, where)
        return 0

    lax.fori_loop(0, nb, fill, 0)

    def chunk_loop(n, step):
        size = 64
        while size * n > 512 and size > 16:
            size //= 2

        def run(i, _):
            step(pl.ds(pl.multiple_of(i * size, size), size))
            return 0

        lax.fori_loop(0, GROUP * BLK // size, run, 0, unroll=2)

    def lanes(t):
        return slice(t * BLK, (t + 1) * BLK)

    def total_of(tiles):
        tiles = list(tiles)
        while len(tiles) > 1:
            pairs = [a + b for a, b in zip(tiles[::2], tiles[1::2])]
            tiles = pairs + tiles[len(pairs) * 2:]
        return jnp.sum(tiles[0], axis=1, keepdims=True)

    def probs(h, r, n, base, extra, p_ref):
        width = n * BLK
        s_ref[:, :width] = dot(q_sc[h, r].reshape(GROUP * BLK, HD), kgat[:width], 1, 1)
        keep = None if extra is None else extra.astype(jnp.float32)

        def step(at):
            exp_s = [jnp.exp2(s_ref[at, lanes(t)] * (scale * LOG2E)) for t in range(n)]
            if keep is not None:
                exp_s[3] = exp_s[3] * keep
            total = total_of(exp_s)
            shrink = jnp.where(total > 1.0, 2.0**-8, 1.0)
            inverse = 1.0 / (total * shrink)
            for t in range(n):
                p_ref[at, lanes(t)] = ((exp_s[t] * shrink) * inverse).astype(jnp.bfloat16)

        chunk_loop(n, step)
        dv = dot(g_sc[h, r].reshape(GROUP * BLK, HD).T, p_ref[:, :width], 1, 0)
        for t in range(n):
            terms_of[2 * h][base + t] = dv[:, lanes(t)]

    def grads(h, r, n, base, p_ref):
        width = n * BLK
        s_ref[:, :width] = dot(g_sc[h, r].reshape(GROUP * BLK, HD), vgat[:width], 1, 1)

        def step(at):
            dp = [s_ref[at, lanes(t)] for t in range(n)]
            p = [p_ref[at, lanes(t)].astype(jnp.float32) for t in range(n)]
            delta = total_of([a * b for a, b in zip(p, dp)])
            for t in range(n):
                dsb[at, lanes(t)] = (p[t] * (dp[t] - delta)).astype(jnp.bfloat16)

        chunk_loop(n, step)
        dq = dot(dsb[:, :width], kgat[:width], 1, 0) * scale
        dq_sc[h, r] = dq.astype(jnp.bfloat16).reshape(GROUP, BLK, HD)
        dk = dot(q_sc[h, r].reshape(GROUP * BLK, HD).T, dsb[:, :width], 1, 0)
        for t in range(n):
            terms_of[2 * h + 1][base + t] = dk[:, lanes(t)]

    def rows(phase, h, first, last):
        keys, values = line[2 * h], line[2 * h + 1]

        def pick(ids):
            for s, c in enumerate(ids):
                kgat[lanes(s)] = keys[c]
                if phase:
                    vgat[lanes(s)] = values[c]

        @pl.loop(first, last)
        def _(r):
            b, ids, extra = slots(r)

            @pl.when(b == 0)
            def _():
                pick(range(nb))
                if phase:
                    grads(h, r, nb, 32, p_full)
                else:
                    probs(h, r, nb, 32, None, p_full)

            @pl.when(b != 0)
            def _():
                pick(ids)
                if phase:
                    grads(h, r, NSLOT, r * 8, p_plain.at[r])
                else:
                    probs(h, r, NSLOT, r * 8, extra, p_plain.at[r])

    def terms(u, j, m):
        ref = terms_of[u]
        at = [tab[r * nb + j * 4 + m] for r in range(4)]
        return (ref[at[0]] + ref[at[1]]) + (ref[at[2]] + ref[at[3]])

    def sum_copy(u, d, j):
        part = sums.at[u, d, pl.ds(j * 4, 4)]
        return rcopy(part, part, rs_s.at[u, d, j], rs_r.at[u, d, j], left if d else right)

    def add_own(u, d, j, first):
        @pl.loop(0, 4)
        def _(m):
            total = terms(u, j, m)
            if not first:
                total = total + sums[u, d, j * 4 + m].astype(jnp.float32)
            sums[u, d, j * 4 + m] = total.astype(jnp.bfloat16)

    def place(d, t):
        i = nz - 1 - z if d else z
        to = i + nz - 1 - t
        return i, nz - 1 - to if d else to

    def sum_step(u, t):
        for d in range(2):
            i, j = place(d, t)

            @pl.when(i == 0)
            def _():
                add_own(u, d, j, True)
                sum_copy(u, d, j).start()

            if t:
                @pl.when((i > 0) & (i <= t))
                def _():
                    sum_copy(u, d, j).wait_recv()
                    add_own(u, d, j, False)
                    sum_copy(u, d, j).start()

    def sum_sends(u):
        for t in range(nz - 1):
            for d in range(2):
                i, j = place(d, t)

                @pl.when(i <= t)
                def _():
                    sum_copy(u, d, j).wait_send()

    def finish(u):
        @pl.when(has_left)
        def _():
            sum_copy(u, 0, z).wait_recv()

        @pl.when(has_right)
        def _():
            sum_copy(u, 1, z).wait_recv()

        out = dk_out if u % 2 else dv_out
        mine = cols(core * 2 + u // 2)

        @pl.loop(0, 4)
        def _(m):
            total = terms(u, z, m)
            at_left = sums[u, 0, z * 4 + m].astype(jnp.float32)
            at_right = sums[u, 1, z * 4 + m].astype(jnp.float32)
            total = total + jnp.where(has_left, at_left, 0.0)
            total = total + jnp.where(has_right, at_right, 0.0)
            if u % 2:
                total = total * scale
            fin[u, m] = total.T.astype(jnp.bfloat16)

        for b in range(2):
            rcopy(
                fin.at[u, other * 2 + b], out.at[block(b), mine], out_s.at[u], out_r.at[u], partner
            ).start()
        for b in range(2):
            out[block(b), mine] = fin[u, core * 2 + b]

    def finish_all(u):
        part = fin.at[u, pl.ds(0, 2)]
        return rcopy(part, part, out_s.at[u], out_r.at[u], partner)

    def dq_back(h):
        for b in range(2):
            for g in range(GROUP):
                at = cols((core * 2 + h) * GROUP + g)
                rcopy(
                    dq_sc.at[h, other * 2 + b, g], dq_out.at[block(b), at],
                    dq_s.at[h], dq_r.at[h], partner,
                ).start()
        for b in range(2):
            for g in range(GROUP):
                at = cols((core * 2 + h) * GROUP + g)
                dq_out[block(b), at] = dq_sc[h, core * 2 + b, g]

    def dq_back_all(h):
        part = dq_sc.at[h, pl.ds(0, 2)]
        return rcopy(part, part, dq_s.at[h], dq_r.at[h], partner)

    def middle(fn, u):
        for dist in range(2, nz - 1):
            fn(u, dist)

    def last(u):
        if nz > 2:
            hop(u, nz - 1)

    def sum_middle(u):
        for t in range(1, nz - 2):
            sum_step(u, t)

    def sum_last(u):
        if nz > 2:
            sum_step(u, nz - 2)

    hop(0, 1)
    middle(hop, 0)
    send_own(1)
    last(0)
    hop(1, 1)
    for h in range(2):
        swap_q_all(h).wait_recv()
    for c in range(2):
        hand_off_all(0, c).wait_recv()
    hand_off(1)
    rows(0, 0, 0, 2)
    middle(hop, 1)
    send_own(2)
    rows(0, 0, 2, 4)
    last(1)
    hop(2, 1)
    sum_step(0, 0)
    rows(1, 0, 0, 2)
    middle(hop, 2)
    send_own(3)
    sum_middle(0)
    rows(1, 0, 2, 4)
    last(2)
    hop(3, 1)
    sum_last(0)
    sum_step(1, 0)
    dq_back(0)
    for c in range(2):
        hand_off_all(1, c).wait_recv()
    rows(0, 1, 0, 2)
    middle(hop, 3)
    sum_middle(1)
    rows(0, 1, 2, 4)
    last(3)
    sum_last(1)
    sum_step(2, 0)
    finish(0)
    rows(1, 1, 0, 2)
    sum_middle(2)
    rows(1, 1, 2, 4)
    sum_last(2)
    sum_step(3, 0)
    dq_back(1)
    finish(1)
    sum_middle(3)
    finish(2)
    sum_last(3)
    finish(3)

    for u in range(4):
        swap_kv_all(u).wait_send()
        hop_sends(u)
        sum_sends(u)
        finish_all(u).wait()
    for h in range(2):
        swap_q_all(h).wait_send()
        for c in range(2):
            hand_off_all(h, c).wait_send()
        dq_back_all(h).wait()


def per_device(n_seg, n_ctx, queries, keys, values, grad_slab, plan, random_blocks):
    nz = n_ctx // 2
    nb = nz * 4
    mb = plan[0]
    query_now = lax.dynamic_index_in_dim(queries[0], mb, 0, keepdims=False)
    key_now = lax.dynamic_index_in_dim(keys[0], mb, 0, keepdims=False)
    value_now = lax.dynamic_index_in_dim(values[0], mb, 0, keepdims=False)
    low = jnp.bfloat16
    vmem = pl.BlockSpec(memory_space=pltpu.VMEM)
    dma = pltpu.SemaphoreType.DMA
    rows4 = pltpu.VMEM((2, 4, GROUP, BLK, HD), low)
    line = pltpu.VMEM((nb, BLK, HD), low)
    tiles = pltpu.VMEM((32 + nb, BLK, HD), jnp.float32)
    wide = pltpu.VMEM((GROUP * BLK, nb * BLK), low)
    dq, dk, dv = pl.pallas_call(
        functools.partial(kernel, n_seg, nz),
        out_shape=(
            jax.ShapeDtypeStruct(query_now.shape, low),
            jax.ShapeDtypeStruct(key_now.shape, low),
            jax.ShapeDtypeStruct(value_now.shape, low),
        ),
        in_specs=[
            pl.BlockSpec(memory_space=pltpu.SMEM), vmem, pl.BlockSpec(memory_space=pl.ANY), vmem,
            vmem,
        ],
        out_specs=(vmem, vmem, vmem),
        scratch_shapes=[
            rows4, rows4, rows4, line, line, line, line, tiles, tiles, tiles, tiles,
            pltpu.VMEM((4, 2, nb, BLK, HD), low), pltpu.VMEM((4, 4, BLK, HD), low),
            pltpu.VMEM((nb * BLK, HD), low), pltpu.VMEM((nb * BLK, HD), low),
            pltpu.VMEM((GROUP * BLK, nb * BLK), jnp.float32), wide,
            pltpu.VMEM((4, GROUP * BLK, NSLOT * BLK), low), wide,
            pltpu.SMEM((4 * nb,), jnp.int32),
            dma((4,)), dma((4,)), dma((2,)), dma((2,)), dma((2, 2)), dma((2, 2)),
            dma((4, 2, nz)), dma((4, nz)), dma((4, 2, nz)), dma((4, 2, nz)),
            dma((2,)), dma((2,)), dma((4,)), dma((4,)),
        ],
        compiler_params=pltpu.CompilerParams(
            collective_id=0, has_side_effects=True, vmem_limit_bytes=60 * 1024 * 1024
        ),
        cost_estimate=pl.CostEstimate(
            flops=6_000_000_000, bytes_accessed=8_000_000, transcendentals=6_000_000
        ),
    )(random_blocks, query_now, grad_slab, key_now, value_now)
    return (dq[None], dk[None], dv[None])


def solution(mesh):
    return jax.shard_map(
        functools.partial(per_device, mesh.shape["segment"], mesh.shape["ctx"]),
        mesh=mesh,
        in_specs=(
            P("segment", None, "ctx", None),
            P("segment", None, "ctx", None),
            P("segment", None, "ctx", None),
            P("segment", "ctx", None),
            P("segment"),
            P(),
        ),
        out_specs=(P("segment", "ctx", None), P("segment", "ctx", None), P("segment", "ctx", None)),
        check_vma=False,
    )
```

```python
import functools

import jax
import jax.numpy as jnp
from jax import lax
from jax.experimental import pallas as pl
from jax.experimental.pallas import tpu as pltpu
from jax.sharding import PartitionSpec as P

HD = 128
BLK = 128
GROUP = 4
NSLOT = 7
LOG2E = 1.4426950408889634
MESH = pl.DeviceIdType.MESH


def dot(a, b, ca, cb):
    return lax.dot_general(a, b, (((ca,), (cb,)), ((), ())), preferred_element_type=jnp.float32)


def kernel(
    n_seg, nz, rb_in, q_in, g_in, k_in, v_in, dq_out, dk_out, dv_out,
    q_sc, g_sc, dq_sc, k0, v0, k1, v1, slv0, slk0, slv1, slk1, sums, fin,
    kgat, vgat, s_ref, dsb, p_plain, p_full, q_t, g_t, tab, rb_ref, rb_sem,
    swap_s, swap_r, qs_s, qs_r, grad_s, grad_r, ga_s, ga_r, rs_s, rs_r,
    dq_s, dq_r, out_s, out_r,
):
    seg = lax.axis_index("segment")
    ctx = lax.axis_index("ctx")
    z = ctx // 2
    core = ctx % 2
    other = 1 - core
    nb = nz * 4
    line = (k0, v0, k1, v1)
    terms_of = (slv0, slk0, slv1, slk1)
    scale = HD ** (-0.5)
    partner = (seg, ctx + 1 - 2 * core)
    right = (seg, ctx + 2)
    left = (seg, ctx - 2)
    ahead = lax.rem(seg + 1, n_seg)
    behind = lax.rem(seg + n_seg - 1, n_seg)
    has_left, has_right = z > 0, z < nz - 1

    def rcopy(src, dst, ss, rs, dev):
        return pltpu.make_async_remote_copy(
            src_ref=src, dst_ref=dst, send_sem=ss, recv_sem=rs, device_id=dev, device_id_type=MESH
        )

    def cols(at):
        return pl.ds(pl.multiple_of(at * HD, HD), HD)

    def block(b):
        return pl.ds(b * BLK, BLK)

    fetch = pltpu.make_async_copy(rb_in, rb_ref, rb_sem)
    fetch.start()

    barrier = pltpu.get_barrier_semaphore()
    for dev in (
        partner, (ahead, z * 2), (ahead, z * 2 + 1), (behind, z * 2), (behind, z * 2 + 1)
    ):
        pl.semaphore_signal(barrier, inc=1, device_id=dev, device_id_type=MESH)

    for j in range(nz):
        @pl.when(z != j)
        def _():
            pl.semaphore_signal(barrier, inc=1, device_id=(seg, j * 2 + core), device_id_type=MESH)

    pl.semaphore_wait(barrier, nz + 4)

    def swap_kv(u):
        source = v_in if u % 2 else k_in
        for b in range(2):
            rcopy(
                source.at[block(b), cols(other * 2 + u // 2)], line[u].at[z * 4 + core * 2 + b],
                swap_s.at[u], swap_r.at[u], partner,
            ).start()

    def swap_kv_all(u):
        part = line[u].at[pl.ds(z * 4 + other * 2, 2)]
        return rcopy(part, part, swap_s.at[u], swap_r.at[u], partner)

    def swap_q(h):
        for b in range(2):
            for g in range(GROUP):
                rcopy(
                    q_in.at[block(b), cols((other * 2 + h) * GROUP + g)],
                    q_sc.at[h, core * 2 + b, g], qs_s.at[h], qs_r.at[h], partner,
                ).start()

    def swap_q_all(h):
        part = q_sc.at[h, pl.ds(other * 2, 2)]
        return rcopy(part, part, qs_s.at[h], qs_r.at[h], partner)

    def hand_off(h):
        for c in range(2):
            for b in range(2):
                for g in range(GROUP):
                    rcopy(
                        g_in.at[0, block(b), cols((c * 2 + h) * GROUP + g)],
                        g_sc.at[h, core * 2 + b, g],
                        grad_s.at[h, c], grad_r.at[h, core], (behind, z * 2 + c),
                    ).start()

    def hand_off_all(h, c):
        part = g_sc.at[h, pl.ds(c * 2, 2)]
        return rcopy(part, part, grad_s.at[h, c], grad_r.at[h, c], (ahead, z * 2 + c))

    def chunk_copy(u, d, j):
        part = line[u].at[pl.ds(j * 4, 4)]
        return rcopy(part, part, ga_s.at[u, d, j], ga_r.at[u, j], left if d else right)

    def direct_copy(j):
        part = line[0].at[pl.ds(z * 4, 4)]
        return rcopy(part, part, ga_s.at[0, 0, j], ga_r.at[0, z], (seg, j * 2 + core))

    def direct_in(j):
        part = line[0].at[pl.ds(j * 4, 4)]
        return rcopy(part, part, ga_s.at[0, 0, j], ga_r.at[0, j], (seg, j * 2 + core))

    def by_distance(fn, dists):
        for dist in dists:
            @pl.when(z + dist < nz)
            def _():
                fn(z + dist)

            @pl.when(z >= dist)
            def _():
                fn(z - dist)

    def send_own(u):
        swap_kv_all(u).wait_recv()

        @pl.when(has_right)
        def _():
            chunk_copy(u, 0, z).start()

        @pl.when(has_left)
        def _():
            chunk_copy(u, 1, z).start()

    def hop(u, dist):
        @pl.when(z >= dist)
        def _():
            chunk_copy(u, 0, z - dist).wait_recv()

            @pl.when(has_right)
            def _():
                chunk_copy(u, 0, z - dist).start()

        @pl.when(z + dist <= nz - 1)
        def _():
            chunk_copy(u, 1, z + dist).wait_recv()

            @pl.when(has_left)
            def _():
                chunk_copy(u, 1, z + dist).start()

    def hop_sends(u):
        for dist in range(nz):
            @pl.when((z >= dist) & has_right)
            def _():
                chunk_copy(u, 0, z - dist).wait_send()

            @pl.when((z + dist <= nz - 1) & has_left)
            def _():
                chunk_copy(u, 1, z + dist).wait_send()

    swap_kv(0)
    hand_off(0)
    swap_q(0)
    for u in range(4):
        source = v_in if u % 2 else k_in
        if u:
            swap_kv(u)
        for b in range(2):
            line[u][z * 4 + core * 2 + b] = source[block(b), cols(core * 2 + u // 2)]
        if u == 0:
            swap_kv_all(0).wait_recv()
            by_distance(lambda j: direct_copy(j).start(), range(nz - 1, 0, -1))
    swap_q(1)
    for h in range(2):
        for b in range(2):
            for g in range(GROUP):
                q_sc[h, core * 2 + b, g] = q_in[block(b), cols((core * 2 + h) * GROUP + g)]

    for u in range(4):
        terms_of[u][NSLOT] = jnp.zeros((BLK, HD), jnp.float32)

    def slots(r):
        b = z * 4 + r
        ids = [lax.rem(b + nb - 1, nb), b, lax.rem(b + 1, nb), 0]
        ids += [rb_ref[i, b] for i in range(3)]
        extra = (b != 0) & (b != 1) & (b != nb - 1)
        return b, ids, extra

    def fill(c, _):
        for r in range(4):
            b, ids, extra = slots(r)
            where = jnp.where(extra & (c == 0), r * 8 + 3, NSLOT)
            for s in (0, 1, 2, 4, 5, 6):
                where = jnp.where(ids[s] == c, r * 8 + s, where)
            tab[r * nb + c] = jnp.where(b == 0, 32 + c, where)
        return 0

    fetch.wait()
    lax.fori_loop(0, nb, fill, 0)

    def turn(src, dst, h):
        @pl.loop(0, 4)
        def _(r):
            dst[h, r] = src[h, r].reshape(GROUP * BLK, HD).T

    def chunk_loop(n, step):
        size = 32 if n <= 8 else 16

        def run(i, _):
            step(pl.ds(pl.multiple_of(i * size, size), size))
            return 0

        lax.fori_loop(0, GROUP * BLK // size, run, 0, unroll=4)

    def lanes(t):
        return slice(t * BLK, (t + 1) * BLK)

    def total_of(tiles):
        tiles = list(tiles)
        while len(tiles) > 1:
            pairs = [a + b for a, b in zip(tiles[::2], tiles[1::2])]
            tiles = pairs + tiles[len(pairs) * 2:]
        return jnp.sum(tiles[0], axis=1, keepdims=True)

    def probs(h, r, n, base, extra, p_ref):
        width = n * BLK
        s_ref[:, :width] = dot(q_sc[h, r].reshape(GROUP * BLK, HD), kgat[:width], 1, 1)
        keep = None if extra is None else extra.astype(jnp.float32)

        def step(at):
            exp_s = [jnp.exp2(s_ref[at, lanes(t)] * (scale * LOG2E)) for t in range(n)]
            if keep is not None:
                exp_s[3] = exp_s[3] * keep
            total = total_of(exp_s)
            shrink = jnp.where(total > 1.0, 2.0**-8, 1.0)
            inverse = 1.0 / (total * shrink)
            for t in range(n):
                p_ref[at, lanes(t)] = ((exp_s[t] * shrink) * inverse).astype(jnp.bfloat16)

        chunk_loop(n, step)
        dv = dot(g_t[h, r], p_ref[:, :width], 1, 0)
        for t in range(n):
            terms_of[2 * h][base + t] = dv[:, lanes(t)]

    def grads(h, r, n, base, p_ref):
        width = n * BLK
        s_ref[:, :width] = dot(g_sc[h, r].reshape(GROUP * BLK, HD), vgat[:width], 1, 1)

        def step(at):
            dp = [s_ref[at, lanes(t)] for t in range(n)]
            p = [p_ref[at, lanes(t)].astype(jnp.float32) for t in range(n)]
            delta = total_of([a * b for a, b in zip(p, dp)])
            for t in range(n):
                dsb[at, lanes(t)] = (p[t] * (dp[t] - delta)).astype(jnp.bfloat16)

        chunk_loop(n, step)
        dq = dot(dsb[:, :width], kgat[:width], 1, 0) * scale
        dq_sc[h, r] = dq.astype(jnp.bfloat16).reshape(GROUP, BLK, HD)
        dk = dot(q_t[h, r], dsb[:, :width], 1, 0)
        for t in range(n):
            terms_of[2 * h + 1][base + t] = dk[:, lanes(t)]

    def rows(phase, h, first, last):
        keys, values = line[2 * h], line[2 * h + 1]

        def pick(ids):
            for s, c in enumerate(ids):
                kgat[lanes(s)] = keys[c]
                if phase:
                    vgat[lanes(s)] = values[c]

        @pl.loop(first, last)
        def _(r):
            b, ids, extra = slots(r)

            @pl.when(b == 0)
            def _():
                pick(range(nb))
                if phase:
                    grads(h, r, nb, 32, p_full)
                else:
                    probs(h, r, nb, 32, None, p_full)

            @pl.when(b != 0)
            def _():
                pick(ids)
                if phase:
                    grads(h, r, NSLOT, r * 8, p_plain.at[r])
                else:
                    probs(h, r, NSLOT, r * 8, extra, p_plain.at[r])

    def terms(u, j, m):
        ref = terms_of[u]
        at = [tab[r * nb + j * 4 + m] for r in range(4)]
        return (ref[at[0]] + ref[at[1]]) + (ref[at[2]] + ref[at[3]])

    def sum_copy(u, d, j):
        part = sums.at[u, d, pl.ds(j * 4, 4)]
        return rcopy(part, part, rs_s.at[u, d, j], rs_r.at[u, d, j], left if d else right)

    def add_own(u, d, j, first):
        @pl.loop(0, 4)
        def _(m):
            total = terms(u, j, m)
            if not first:
                total = total + sums[u, d, j * 4 + m].astype(jnp.float32)
            sums[u, d, j * 4 + m] = total.astype(jnp.bfloat16)

    def place(d, t):
        i = nz - 1 - z if d else z
        to = i + nz - 1 - t
        return i, nz - 1 - to if d else to

    def sum_step(u, t):
        for d in range(2):
            i, j = place(d, t)

            @pl.when(i == 0)
            def _():
                add_own(u, d, j, True)
                sum_copy(u, d, j).start()

            if t:
                @pl.when((i > 0) & (i <= t))
                def _():
                    sum_copy(u, d, j).wait_recv()
                    add_own(u, d, j, False)
                    sum_copy(u, d, j).start()

    def sum_sends(u):
        for t in range(nz - 1):
            for d in range(2):
                i, j = place(d, t)

                @pl.when(i <= t)
                def _():
                    sum_copy(u, d, j).wait_send()

    def owner_copy(j):
        return rcopy(
            sums.at[3, 0, pl.ds(j * 4, 4)], sums.at[3, 1, pl.ds(z * 4, 4)],
            rs_s.at[3, 0, j], rs_r.at[3, 1, z], (seg, j * 2 + core),
        )

    def owner_in(j):
        part = sums.at[3, 1, pl.ds(j * 4, 4)]
        return rcopy(part, part, rs_s.at[3, 0, j], rs_r.at[3, 1, j], (seg, j * 2 + core))

    def to_owner(j):
        add_own(3, 0, j, True)
        owner_copy(j).start()

    def finish(u):
        if u == 3:
            by_distance(lambda j: owner_in(j).wait_recv(), range(1, nz))
        else:
            @pl.when(has_left)
            def _():
                sum_copy(u, 0, z).wait_recv()

            @pl.when(has_right)
            def _():
                sum_copy(u, 1, z).wait_recv()

        out = dk_out if u % 2 else dv_out
        mine = cols(core * 2 + u // 2)

        @pl.loop(0, 4)
        def _(m):
            total = terms(u, z, m)
            if u == 3:
                parts = [(z != j, sums[3, 1, j * 4 + m]) for j in range(nz)]
            else:
                parts = [(has_left, sums[u, 0, z * 4 + m]), (has_right, sums[u, 1, z * 4 + m])]
            for there, part in parts:
                total = total + jnp.where(there, part.astype(jnp.float32), 0.0)
            if u % 2:
                total = total * scale
            fin[u, m] = total.T.astype(jnp.bfloat16)

        for b in range(2):
            rcopy(
                fin.at[u, other * 2 + b], out.at[block(b), mine], out_s.at[u], out_r.at[u], partner
            ).start()
        for b in range(2):
            out[block(b), mine] = fin[u, core * 2 + b]

    def finish_all(u):
        part = fin.at[u, pl.ds(0, 2)]
        return rcopy(part, part, out_s.at[u], out_r.at[u], partner)

    def dq_back(h):
        for b in range(2):
            for g in range(GROUP):
                at = cols((core * 2 + h) * GROUP + g)
                rcopy(
                    dq_sc.at[h, other * 2 + b, g], dq_out.at[block(b), at],
                    dq_s.at[h], dq_r.at[h], partner,
                ).start()
        for b in range(2):
            for g in range(GROUP):
                at = cols((core * 2 + h) * GROUP + g)
                dq_out[block(b), at] = dq_sc[h, core * 2 + b, g]

    def dq_back_all(h):
        part = dq_sc.at[h, pl.ds(0, 2)]
        return rcopy(part, part, dq_s.at[h], dq_r.at[h], partner)

    def middle(fn, u):
        for dist in range(2, nz - 1):
            fn(u, dist)

    def last(u):
        if nz > 2:
            hop(u, nz - 1)

    def sum_middle(u):
        for t in range(1, nz - 2):
            sum_step(u, t)

    def sum_last(u):
        if nz > 2:
            sum_step(u, nz - 2)

    by_distance(lambda j: direct_in(j).wait_recv(), [1])
    send_own(1)
    for h in range(2):
        swap_q_all(h).wait_recv()
        turn(q_sc, q_t, h)
    for c in range(2):
        hand_off_all(0, c).wait_recv()
    hand_off(1)
    turn(g_sc, g_t, 0)
    by_distance(lambda j: direct_in(j).wait_recv(), range(2, nz))
    hop(1, 1)
    send_own(2)
    rows(0, 0, 0, 2)
    middle(hop, 1)
    hop(2, 1)
    send_own(3)
    rows(0, 0, 2, 4)
    last(1)
    middle(hop, 2)
    hop(3, 1)
    sum_step(0, 0)
    rows(1, 0, 0, 2)
    last(2)
    middle(hop, 3)
    rows(1, 0, 2, 4)
    last(3)
    sum_middle(0)
    sum_step(1, 0)
    dq_back(0)
    for c in range(2):
        hand_off_all(1, c).wait_recv()
    turn(g_sc, g_t, 1)
    rows(0, 1, 0, 2)
    sum_last(0)
    rows(0, 1, 2, 4)
    sum_middle(1)
    sum_step(2, 0)
    rows(1, 1, 0, 2)
    sum_last(1)
    rows(1, 1, 2, 4)
    by_distance(to_owner, range(nz - 1, 0, -1))
    dq_back(1)
    sum_middle(2)
    finish(0)
    sum_last(2)
    finish(1)
    finish(2)
    finish(3)

    by_distance(lambda j: direct_copy(j).wait_send(), range(1, nz))
    by_distance(lambda j: owner_copy(j).wait_send(), range(1, nz))
    for u in range(4):
        swap_kv_all(u).wait_send()
        if u:
            hop_sends(u)
        if u < 3:
            sum_sends(u)
        finish_all(u).wait()
    for h in range(2):
        swap_q_all(h).wait_send()
        for c in range(2):
            hand_off_all(h, c).wait_send()
        dq_back_all(h).wait()


def move(pairs, sem):
    copies = []
    for i, (src, dst) in enumerate(pairs):
        rows = src.shape[0] // 4
        for n in range(4):
            at = pl.ds(n * rows, rows)
            copies.append(pltpu.make_async_copy(src.at[at], dst.at[at], sem.at[i, n]))
    for copy in copies:
        copy.start()
    for copy in copies:
        copy.wait()


def pick_batch(plan_ref, q_all, k_all, v_all, q_out, k_out, v_out, sem):
    mb = plan_ref[0]
    sources = [ref.at[0, mb] for ref in (q_all, k_all, v_all)]
    move(zip(sources, (q_out, k_out, v_out)), sem)


def hand_out(dq_in, dk_in, dv_in, dq_out, dk_out, dv_out, sem):
    targets = [ref.at[0] for ref in (dq_out, dk_out, dv_out)]
    move(zip((dq_in, dk_in, dv_in), targets), sem)


def per_device(n_seg, n_ctx, queries, keys, values, grad_slab, plan, random_blocks):
    nz = n_ctx // 2
    nb = nz * 4
    low = jnp.bfloat16
    vmem = pl.BlockSpec(memory_space=pltpu.VMEM)
    hbm = pl.BlockSpec(memory_space=pl.ANY)
    smem = pl.BlockSpec(memory_space=pltpu.SMEM)
    dma = pltpu.SemaphoreType.DMA
    query_now, key_now, value_now = pl.pallas_call(
        pick_batch,
        out_shape=tuple(
            jax.ShapeDtypeStruct(a.shape[2:], low) for a in (queries, keys, values)
        ),
        in_specs=[smem, hbm, hbm, hbm],
        out_specs=(hbm, hbm, hbm),
        scratch_shapes=[dma((3, 4))],
        compiler_params=pltpu.CompilerParams(vmem_limit_bytes=60 * 1024 * 1024),
    )(plan, queries, keys, values)
    rows4 = pltpu.VMEM((2, 4, GROUP, BLK, HD), low)
    rows_t = pltpu.VMEM((2, 4, HD, GROUP * BLK), low)
    line = pltpu.VMEM((nb, BLK, HD), low)
    tiles = pltpu.VMEM((32 + nb, BLK, HD), jnp.float32)
    wide = pltpu.VMEM((GROUP * BLK, nb * BLK), low)
    dq, dk, dv = pl.pallas_call(
        functools.partial(kernel, n_seg, nz),
        out_shape=(
            jax.ShapeDtypeStruct(query_now.shape, low),
            jax.ShapeDtypeStruct(key_now.shape, low),
            jax.ShapeDtypeStruct(value_now.shape, low),
        ),
        in_specs=[hbm, vmem, hbm, vmem, vmem],
        out_specs=(vmem, vmem, vmem),
        scratch_shapes=[
            rows4, rows4, rows4, line, line, line, line, tiles, tiles, tiles, tiles,
            pltpu.VMEM((4, 2, nb, BLK, HD), low), pltpu.VMEM((4, 4, BLK, HD), low),
            pltpu.VMEM((nb * BLK, HD), low), pltpu.VMEM((nb * BLK, HD), low),
            pltpu.VMEM((GROUP * BLK, nb * BLK), jnp.float32), wide,
            pltpu.VMEM((4, GROUP * BLK, NSLOT * BLK), low), wide,
            rows_t, rows_t, pltpu.SMEM((4 * nb,), jnp.int32),
            pltpu.SMEM(random_blocks.shape[::-1], jnp.int32), dma,
            dma((4,)), dma((4,)), dma((2,)), dma((2,)), dma((2, 2)), dma((2, 2)),
            dma((4, 2, nz)), dma((4, nz)), dma((4, 2, nz)), dma((4, 2, nz)),
            dma((2,)), dma((2,)), dma((4,)), dma((4,)),
        ],
        compiler_params=pltpu.CompilerParams(
            collective_id=0, has_side_effects=True, vmem_limit_bytes=60 * 1024 * 1024
        ),
        cost_estimate=pl.CostEstimate(
            flops=6_000_000_000, bytes_accessed=8_000_000, transcendentals=6_000_000
        ),
    )(random_blocks.T, query_now, grad_slab, key_now, value_now)
    outs = (dq, dk, dv)
    return pl.pallas_call(
        hand_out,
        out_shape=tuple(jax.ShapeDtypeStruct((1,) + a.shape, low) for a in outs),
        in_specs=[hbm, hbm, hbm],
        out_specs=(hbm, hbm, hbm),
        scratch_shapes=[dma((3, 4))],
        compiler_params=pltpu.CompilerParams(vmem_limit_bytes=60 * 1024 * 1024),
    )(*outs)


def solution(mesh):
    return jax.shard_map(
        functools.partial(per_device, mesh.shape["segment"], mesh.shape["ctx"]),
        mesh=mesh,
        in_specs=(
            P("segment", None, "ctx", None),
            P("segment", None, "ctx", None),
            P("segment", None, "ctx", None),
            P("segment", "ctx", None),
            P("segment"),
            P(),
        ),
        out_specs=(P("segment", "ctx", None), P("segment", "ctx", None), P("segment", "ctx", None)),
        check_vma=False,
    )
```

```python
import functools

import jax
import jax.numpy as jnp
from jax import lax
from jax.experimental import pallas as pl
from jax.experimental.pallas import tpu as pltpu
from jax.sharding import PartitionSpec as P

HD = 128
BLK = 128
GROUP = 4
NSLOT = 7
LOG2E = 1.4426950408889634
MESH = pl.DeviceIdType.MESH


def dot(a, b, ca, cb):
    return lax.dot_general(a, b, (((ca,), (cb,)), ((), ())), preferred_element_type=jnp.float32)


def kernel(
    n_seg, nz, rb_in, q_in, g_in, k_in, v_in, dq_out, dk_out, dv_out,
    q_sc, g_sc, dq_sc, k0, v0, k1, v1, slv0, slk0, slv1, slk1, sums, fin,
    kgat, vgat, s_ref, p_plain, p_full, q_t, g_t, q_own, g_own, kv_own, dq_box, tab, rb_ref,
    rb_sem,
    swap_s, swap_r, qs_s, qs_r, grad_s, grad_r, ga_s, ga_r, rs_s, rs_r,
    dq_s, dq_r, out_s, out_r,
):
    seg = lax.axis_index("segment")
    ctx = lax.axis_index("ctx")
    z = ctx // 2
    core = ctx % 2
    other = 1 - core
    nb = nz * 4
    line = (k0, v0, k1, v1)
    terms_of = (slv0, slk0, slv1, slk1)
    scale = HD ** (-0.5)
    partner = (seg, ctx + 1 - 2 * core)
    right = (seg, ctx + 2)
    left = (seg, ctx - 2)
    ahead = lax.rem(seg + 1, n_seg)
    behind = lax.rem(seg + n_seg - 1, n_seg)
    has_left, has_right = z > 0, z < nz - 1

    def rcopy(src, dst, ss, rs, dev):
        return pltpu.make_async_remote_copy(
            src_ref=src, dst_ref=dst, send_sem=ss, recv_sem=rs, device_id=dev, device_id_type=MESH
        )

    def cols(at):
        return pl.ds(pl.multiple_of(at * HD, HD), HD)

    def lanes(t):
        return slice(t * BLK, (t + 1) * BLK)

    def block(b):
        return pl.ds(b * BLK, BLK)

    fetch = pltpu.make_async_copy(rb_in, rb_ref, rb_sem)
    fetch.start()

    barrier = pltpu.get_barrier_semaphore()
    for dev in (
        partner, (ahead, z * 2), (ahead, z * 2 + 1), (behind, z * 2), (behind, z * 2 + 1)
    ):
        pl.semaphore_signal(barrier, inc=1, device_id=dev, device_id_type=MESH)

    @pl.when(has_left)
    def _():
        pl.semaphore_signal(barrier, inc=1, device_id=left, device_id_type=MESH)

    @pl.when(has_right)
    def _():
        pl.semaphore_signal(barrier, inc=1, device_id=right, device_id_type=MESH)

    pl.semaphore_wait(barrier, 5 + has_left.astype(jnp.int32) + has_right.astype(jnp.int32))

    for b in range(2):
        for j in range(4):
            kv_own[0, j, b] = k_in[block(b), lanes(j)]
            kv_own[1, j, b] = v_in[block(b), lanes(j)]
            for g in range(GROUP):
                g_own[j, b, g] = g_in[0, block(b), lanes(j * GROUP + g)]
                q_own[j, b, g] = q_in[block(b), lanes(j * GROUP + g)]

    def swap_kv(u):
        return rcopy(
            kv_own.at[u % 2, other * 2 + u // 2], line[u].at[pl.ds(z * 4 + core * 2, 2)],
            swap_s.at[u], swap_r.at[u], partner,
        )

    def swap_kv_all(u):
        part = line[u].at[pl.ds(z * 4 + other * 2, 2)]
        return rcopy(part, part, swap_s.at[u], swap_r.at[u], partner)

    def swap_q(h):
        return rcopy(
            q_own.at[other * 2 + h], q_sc.at[h, pl.ds(core * 2, 2)],
            qs_s.at[h], qs_r.at[h], partner,
        )

    def swap_q_all(h):
        part = q_sc.at[h, pl.ds(other * 2, 2)]
        return rcopy(part, part, qs_s.at[h], qs_r.at[h], partner)

    def hand_off(h):
        for c in range(2):
            rcopy(
                g_own.at[c * 2 + h], g_sc.at[h, pl.ds(core * 2, 2)],
                grad_s.at[h, c], grad_r.at[h, core], (behind, z * 2 + c),
            ).start()

    def hand_off_all(h, c):
        part = g_sc.at[h, pl.ds(c * 2, 2)]
        return rcopy(part, part, grad_s.at[h, c], grad_r.at[h, c], (ahead, z * 2 + c))

    def chunk_copy(u, d, j):
        part = line[u].at[pl.ds(j * 4, 4)]
        return rcopy(part, part, ga_s.at[u, d, j], ga_r.at[u, j], left if d else right)

    def send_own(u):
        swap_kv_all(u).wait_recv()

        @pl.when(has_right)
        def _():
            chunk_copy(u, 0, z).start()

        @pl.when(has_left)
        def _():
            chunk_copy(u, 1, z).start()

    def hop(u, dist):
        @pl.when(z >= dist)
        def _():
            chunk_copy(u, 0, z - dist).wait_recv()

            @pl.when(has_right)
            def _():
                chunk_copy(u, 0, z - dist).start()

        @pl.when(z + dist <= nz - 1)
        def _():
            chunk_copy(u, 1, z + dist).wait_recv()

            @pl.when(has_left)
            def _():
                chunk_copy(u, 1, z + dist).start()

    def hop_sends(u):
        for dist in range(nz):
            @pl.when((z >= dist) & has_right)
            def _():
                chunk_copy(u, 0, z - dist).wait_send()

            @pl.when((z + dist <= nz - 1) & has_left)
            def _():
                chunk_copy(u, 1, z + dist).wait_send()

    swap_kv(0).start()
    hand_off(0)
    swap_q(0).start()
    for u in range(4):
        if u:
            swap_kv(u).start()
        line[u][pl.ds(z * 4 + core * 2, 2)] = kv_own[u % 2, core * 2 + u // 2]
        if u == 0:
            send_own(0)
    swap_q(1).start()
    for h in range(2):
        q_sc[h, pl.ds(core * 2, 2)] = q_own[core * 2 + h]

    for u in range(4):
        terms_of[u][NSLOT] = jnp.zeros((BLK, HD), jnp.float32)

    def slots(r):
        b = z * 4 + r
        ids = [lax.rem(b + nb - 1, nb), b, lax.rem(b + 1, nb), 0]
        ids += [rb_ref[i, b] for i in range(3)]
        extra = (b != 0) & (b != 1) & (b != nb - 1)
        return b, ids, extra

    def fill(c, _):
        for r in range(4):
            b, ids, extra = slots(r)
            where = jnp.where(extra & (c == 0), r * 8 + 3, NSLOT)
            for s in (0, 1, 2, 4, 5, 6):
                where = jnp.where(ids[s] == c, r * 8 + s, where)
            tab[r * nb + c] = jnp.where(b == 0, 32 + c, where)
        return 0

    fetch.wait()
    lax.fori_loop(0, nb, fill, 0)

    def turn(src, dst, h):
        @pl.loop(0, 4)
        def _(r):
            dst[h, r] = src[h, r].reshape(GROUP * BLK, HD).T

    def chunk_loop(n, step):
        size = 64
        while size * n > 512 and size > 16:
            size //= 2

        def run(i, _):
            step(pl.ds(pl.multiple_of(i * size, size), size))
            return 0

        lax.fori_loop(0, GROUP * BLK // size, run, 0, unroll=2)

    def total_of(tiles):
        tiles = list(tiles)
        while len(tiles) > 1:
            pairs = [a + b for a, b in zip(tiles[::2], tiles[1::2])]
            tiles = pairs + tiles[len(pairs) * 2:]
        return jnp.sum(tiles[0], axis=1, keepdims=True)

    def probs(h, r, n, base, extra, p_ref):
        width = n * BLK
        s_ref[:, :width] = dot(q_sc[h, r].reshape(GROUP * BLK, HD), kgat[:width], 1, 1)
        keep = None if extra is None else extra.astype(jnp.float32)

        def step(at):
            exp_s = [jnp.exp2(s_ref[at, lanes(t)] * (scale * LOG2E)) for t in range(n)]
            if keep is not None:
                exp_s[3] = exp_s[3] * keep
            total = total_of(exp_s)
            shrink = jnp.where(total > 1.0, 2.0**-8, 1.0)
            inverse = 1.0 / (total * shrink)
            for t in range(n):
                p_ref[at, lanes(t)] = ((exp_s[t] * shrink) * inverse).astype(jnp.bfloat16)

        chunk_loop(n, step)
        dv = dot(g_t[h, r], p_ref[:, :width], 1, 0)
        for t in range(n):
            terms_of[2 * h][base + t] = dv[:, lanes(t)]

    def grads(h, r, n, base, p_ref):
        width = n * BLK
        s_ref[:, :width] = dot(g_sc[h, r].reshape(GROUP * BLK, HD), vgat[:width], 1, 1)

        def step(at):
            dp = [s_ref[at, lanes(t)] for t in range(n)]
            p = [p_ref[at, lanes(t)].astype(jnp.float32) for t in range(n)]
            delta = total_of([a * b for a, b in zip(p, dp)])
            for t in range(n):
                p_ref[at, lanes(t)] = (p[t] * (dp[t] - delta)).astype(jnp.bfloat16)

        chunk_loop(n, step)
        dq = dot(p_ref[:, :width], kgat[:width], 1, 0) * scale
        dq_sc[h, r] = dq.astype(jnp.bfloat16).reshape(GROUP, BLK, HD)
        dk = dot(q_t[h, r], p_ref[:, :width], 1, 0)
        for t in range(n):
            terms_of[2 * h + 1][base + t] = dk[:, lanes(t)]

    def rows(phase, h, first, last):
        keys, values = line[2 * h], line[2 * h + 1]

        def pick(ids):
            for s, c in enumerate(ids):
                kgat[lanes(s)] = keys[c]
                if phase:
                    vgat[lanes(s)] = values[c]

        @pl.loop(first, last)
        def _(r):
            b, ids, extra = slots(r)

            @pl.when(b == 0)
            def _():
                pick(range(nb))
                if phase:
                    grads(h, r, nb, 32, p_full)
                else:
                    probs(h, r, nb, 32, None, p_full)

            @pl.when(b != 0)
            def _():
                pick(ids)
                if phase:
                    grads(h, r, NSLOT, r * 8, p_plain.at[r])
                else:
                    probs(h, r, NSLOT, r * 8, extra, p_plain.at[r])

    def terms(u, j, m):
        ref = terms_of[u]
        at = [tab[r * nb + j * 4 + m] for r in range(4)]
        return (ref[at[0]] + ref[at[1]]) + (ref[at[2]] + ref[at[3]])

    def sum_copy(u, d, j):
        part = sums.at[u, d, pl.ds(j * 4, 4)]
        return rcopy(part, part, rs_s.at[u, d, j], rs_r.at[u, d, j], left if d else right)

    def add_own(u, d, j, first):
        @pl.loop(0, 4)
        def _(m):
            total = terms(u, j, m)
            if not first:
                total = total + sums[u, d, j * 4 + m].astype(jnp.float32)
            sums[u, d, j * 4 + m] = total.astype(jnp.bfloat16)

    def place(d, t):
        i = nz - 1 - z if d else z
        to = i + nz - 1 - t
        return i, nz - 1 - to if d else to

    def sum_step(u, t):
        for d in range(2):
            i, j = place(d, t)

            @pl.when(i == 0)
            def _():
                add_own(u, d, j, True)
                sum_copy(u, d, j).start()

            if t:
                @pl.when((i > 0) & (i <= t))
                def _():
                    sum_copy(u, d, j).wait_recv()
                    add_own(u, d, j, False)
                    sum_copy(u, d, j).start()

    def sum_sends(u):
        for t in range(nz - 1):
            for d in range(2):
                i, j = place(d, t)

                @pl.when(i <= t)
                def _():
                    sum_copy(u, d, j).wait_send()

    def finish(u):
        @pl.when(has_left)
        def _():
            sum_copy(u, 0, z).wait_recv()

        @pl.when(has_right)
        def _():
            sum_copy(u, 1, z).wait_recv()

        out = dk_out if u % 2 else dv_out
        mine = cols(core * 2 + u // 2)

        @pl.loop(0, 4)
        def _(m):
            total = terms(u, z, m)
            at_left = sums[u, 0, z * 4 + m].astype(jnp.float32)
            at_right = sums[u, 1, z * 4 + m].astype(jnp.float32)
            total = total + jnp.where(has_left, at_left, 0.0)
            total = total + jnp.where(has_right, at_right, 0.0)
            if u % 2:
                total = total * scale
            fin[u, m] = total.T.astype(jnp.bfloat16)

        for b in range(2):
            rcopy(
                fin.at[u, other * 2 + b], out.at[block(b), mine], out_s.at[u], out_r.at[u], partner
            ).start()
        for b in range(2):
            out[block(b), mine] = fin[u, core * 2 + b]

    def finish_all(u):
        part = fin.at[u, pl.ds(0, 2)]
        return rcopy(part, part, out_s.at[u], out_r.at[u], partner)

    def dq_back(h):
        rcopy(
            dq_sc.at[h, pl.ds(other * 2, 2)], dq_box.at[h], dq_s.at[h], dq_r.at[h], partner
        ).start()
        for b in range(2):
            for g in range(GROUP):
                at = cols((core * 2 + h) * GROUP + g)
                dq_out[block(b), at] = dq_sc[h, core * 2 + b, g]

    def dq_in(h):
        dq_back_all(h).wait()
        for b in range(2):
            for g in range(GROUP):
                at = cols((other * 2 + h) * GROUP + g)
                dq_out[block(b), at] = dq_box[h, b, g]

    def dq_back_all(h):
        part = dq_sc.at[h, pl.ds(0, 2)]
        return rcopy(part, part, dq_s.at[h], dq_r.at[h], partner)

    def middle(fn, u):
        for dist in range(2, nz - 1):
            fn(u, dist)

    def last(u):
        if nz > 2:
            hop(u, nz - 1)

    def sum_middle(u):
        for t in range(1, nz - 2):
            sum_step(u, t)

    def sum_last(u):
        if nz > 2:
            sum_step(u, nz - 2)

    hop(0, 1)
    for h in range(2):
        swap_q_all(h).wait_recv()
    turn(q_sc, q_t, 0)
    middle(hop, 0)
    send_own(1)
    turn(q_sc, q_t, 1)
    last(0)
    hop(1, 1)
    for c in range(2):
        hand_off_all(0, c).wait_recv()
    hand_off(1)
    turn(g_sc, g_t, 0)
    rows(0, 0, 0, 2)
    middle(hop, 1)
    send_own(2)
    rows(0, 0, 2, 4)
    last(1)
    hop(2, 1)
    sum_step(0, 0)
    rows(1, 0, 0, 2)
    middle(hop, 2)
    send_own(3)
    sum_middle(0)
    rows(1, 0, 2, 4)
    last(2)
    hop(3, 1)
    sum_last(0)
    sum_step(1, 0)
    dq_back(0)
    for c in range(2):
        hand_off_all(1, c).wait_recv()
    turn(g_sc, g_t, 1)
    rows(0, 1, 0, 2)
    middle(hop, 3)
    sum_middle(1)
    rows(0, 1, 2, 4)
    last(3)
    sum_last(1)
    sum_step(2, 0)
    finish(0)
    rows(1, 1, 0, 2)
    sum_middle(2)
    rows(1, 1, 2, 4)
    sum_last(2)
    sum_step(3, 0)
    dq_back(1)
    finish(1)
    dq_in(0)
    sum_middle(3)
    finish(2)
    dq_in(1)
    sum_last(3)
    finish(3)

    for u in range(4):
        swap_kv_all(u).wait_send()
        hop_sends(u)
        sum_sends(u)
        finish_all(u).wait()
    for h in range(2):
        swap_q_all(h).wait_send()
        for c in range(2):
            hand_off_all(h, c).wait_send()


def pick_batch(plan_ref, q_all, k_all, v_all, q_out, k_out, v_out, sem):
    mb = plan_ref[0]
    copies = []
    for i, (src, dst) in enumerate(((q_all, q_out), (k_all, k_out), (v_all, v_out))):
        rows = dst.shape[0] // 4
        for n in range(4):
            at = pl.ds(n * rows, rows)
            copies.append(pltpu.make_async_copy(src.at[0, mb, at], dst.at[at], sem.at[i, n]))
    for copy in copies:
        copy.start()
    for copy in copies:
        copy.wait()


def hand_out(dq_in, dk_in, dv_in, dq_out, dk_out, dv_out):
    dq_out[0] = dq_in[...]
    dk_out[0] = dk_in[...]
    dv_out[0] = dv_in[...]


def per_device(n_seg, n_ctx, queries, keys, values, grad_slab, plan, random_blocks):
    nz = n_ctx // 2
    nb = nz * 4
    low = jnp.bfloat16
    vmem = pl.BlockSpec(memory_space=pltpu.VMEM)
    hbm = pl.BlockSpec(memory_space=pl.ANY)
    smem = pl.BlockSpec(memory_space=pltpu.SMEM)
    dma = pltpu.SemaphoreType.DMA
    roomy = pltpu.CompilerParams(vmem_limit_bytes=60 * 1024 * 1024)
    query_now, key_now, value_now = pl.pallas_call(
        pick_batch,
        out_shape=tuple(
            jax.ShapeDtypeStruct(a.shape[2:], low) for a in (queries, keys, values)
        ),
        in_specs=[smem, hbm, hbm, hbm],
        out_specs=(vmem, vmem, vmem),
        scratch_shapes=[dma((3, 4))],
        compiler_params=roomy,
    )(plan, queries, keys, values)
    rows4 = pltpu.VMEM((2, 4, GROUP, BLK, HD), low)
    rows_t = pltpu.VMEM((2, 4, HD, GROUP * BLK), low)
    heads = pltpu.VMEM((4, 2, GROUP, BLK, HD), low)
    line = pltpu.VMEM((nb, BLK, HD), low)
    tiles = pltpu.VMEM((32 + nb, BLK, HD), jnp.float32)
    wide = pltpu.VMEM((GROUP * BLK, nb * BLK), low)
    dq, dk, dv = pl.pallas_call(
        functools.partial(kernel, n_seg, nz),
        out_shape=(
            jax.ShapeDtypeStruct(query_now.shape, low),
            jax.ShapeDtypeStruct(key_now.shape, low),
            jax.ShapeDtypeStruct(value_now.shape, low),
        ),
        in_specs=[hbm, vmem, vmem, vmem, vmem],
        out_specs=(vmem, vmem, vmem),
        scratch_shapes=[
            rows4, rows4, rows4, line, line, line, line, tiles, tiles, tiles, tiles,
            pltpu.VMEM((4, 2, nb, BLK, HD), low), pltpu.VMEM((4, 4, BLK, HD), low),
            pltpu.VMEM((nb * BLK, HD), low), pltpu.VMEM((nb * BLK, HD), low),
            pltpu.VMEM((GROUP * BLK, nb * BLK), jnp.float32),
            pltpu.VMEM((4, GROUP * BLK, NSLOT * BLK), low), wide,
            rows_t, rows_t, heads, heads, pltpu.VMEM((2, 4, 2, BLK, HD), low),
            pltpu.VMEM((2, 2, GROUP, BLK, HD), low),
            pltpu.SMEM((4 * nb,), jnp.int32),
            pltpu.SMEM(random_blocks.shape[::-1], jnp.int32), dma,
            dma((4,)), dma((4,)), dma((2,)), dma((2,)), dma((2, 2)), dma((2, 2)),
            dma((4, 2, nz)), dma((4, nz)), dma((4, 2, nz)), dma((4, 2, nz)),
            dma((2,)), dma((2,)), dma((4,)), dma((4,)),
        ],
        compiler_params=pltpu.CompilerParams(
            collective_id=0, has_side_effects=True, vmem_limit_bytes=60 * 1024 * 1024
        ),
        cost_estimate=pl.CostEstimate(
            flops=6_000_000_000, bytes_accessed=8_000_000, transcendentals=6_000_000
        ),
    )(random_blocks.T, query_now, grad_slab, key_now, value_now)
    outs = (dq, dk, dv)
    return pl.pallas_call(
        hand_out,
        out_shape=tuple(jax.ShapeDtypeStruct((1,) + a.shape, low) for a in outs),
        in_specs=[vmem, vmem, vmem],
        out_specs=(vmem, vmem, vmem),
        compiler_params=roomy,
    )(*outs)


def solution(mesh):
    return jax.shard_map(
        functools.partial(per_device, mesh.shape["segment"], mesh.shape["ctx"]),
        mesh=mesh,
        in_specs=(
            P("segment", None, "ctx", None),
            P("segment", None, "ctx", None),
            P("segment", None, "ctx", None),
            P("segment", "ctx", None),
            P("segment"),
            P(),
        ),
        out_specs=(P("segment", "ctx", None), P("segment", "ctx", None), P("segment", "ctx", None)),
        check_vma=False,
    )
```
